256 devices in a mesh: dp: 16 (over z, core), mp: 16 (over x, y).
Axes of the slice: x: 4, y: 4, z: 8, core: 2. Of those that a mesh axis runs over, the one named last changes fastest.
Arguments:
- tokens: bfloat16 [163840, 8192], P(('dp', 'mp')), may hold values from -24 to 24
- out_grads: bfloat16 [163840, 2, 128], P(('dp', 'mp')), may hold values from -0.0625 to 0.0625
- momentum: float32 [16, 8192, 2, 128], P('dp', 'mp'), may hold values from -6 to 6
- selected: int32 [128, 2, 2, 32], P('mp'), may hold values from 0 to 4095, as said below
Outputs:
- new_momentum: float32 [16, 8192, 2, 128], P('dp', 'mp')
- update: float32 [8192, 2, 128], P('mp')
The draws below stay inside these ranges and needn't reach their ends.
Inputs may be any that keep to these rules, and one draw needn't show every extreme that they name: `selected`: within each span the 32 indices are distinct.
All inputs are finite; a program needn't handle non-finite values.
Results may differ from the reference program's by a relative error of at most 0.0003.
Values sent between devices are 32-bit elements; how exact they have to be, the bound alone decides.
No kernel may reach another device: no remote copies, remote signals or barrier semaphores. Data moves between devices by JAX's collectives and lax.ppermute only.
A program may use at most 128 MiB of HBM per device.

```python
import math
import jax
import jax.numpy as jnp
from jax import lax

D = 8192
FFW = 128
TOK_DEV = 640
SPAN = 64
K = 32
TOKENS = 163840
N_DP = 16
N_MP = 16


def draw_selected(key, part):
    key = jax.random.fold_in(key, 7)
    count = D // SPAN * 2 * (FFW // SPAN)
    keys = jax.random.split(key, count)
    picked = jax.vmap(lambda one: jax.random.permutation(one, SPAN * SPAN)[:K])(keys)
    return picked.reshape(D // SPAN, 2, FFW // SPAN, K).astype(jnp.int32)


def strengthened(array, key, source, target, parts, factor):
    def block_of(dim):
        return (jnp.arange(array.shape[dim]) // (array.shape[dim] // parts)).reshape((-1,) + (1,) * (array.ndim - 1 - dim))

    one_side = jax.random.permutation(key, parts)[block_of(target)]
    other_side = (block_of(target) + parts // 2) % parts
    return jnp.where((block_of(source) == one_side) | (block_of(source) == other_side), factor * array, array)


def steps_of(rng, extent, cuts, least, largest):
    loudness = 1.0
    for dim, shards_of in cuts:
        steps = jax.random.uniform(jax.random.fold_in(jax.random.fold_in(rng, 6), dim), (shards_of,), jnp.float32, least / len(cuts), largest / len(cuts))
        loudness = loudness * jnp.repeat(jnp.exp(steps), extent[dim] // shards_of).reshape((-1,) + (1,) * (len(extent) - 1 - dim))
    return loudness


def gaussian(own_key, dims, scale, reach, cuts=(), kind=jnp.bfloat16):
    drawn = scale * jax.random.normal(own_key, dims, jnp.float32)
    if cuts:
        drawn = drawn * steps_of(own_key, dims, cuts, -0.22, 0.18)
    return jnp.clip(drawn, -reach, reach).astype(kind)


def gaussian_with(key, dims, deviation, most, pieces, heavy, kind=jnp.bfloat16):
    drawn = deviation * jax.random.normal(key, dims, jnp.float32)
    if pieces:
        drawn = drawn * steps_of(key, dims, pieces, -0.22, 0.18)
    return jnp.clip(strengthened(drawn, jax.random.fold_in(key, 3), *heavy), -most, most).astype(kind)


def setup_inputs(seed: int = 0) -> dict:
    splits = jax.random.split(jax.random.key(seed), 5)
    tokens = gaussian_with(splits[0], (TOKENS, D), 1.0, 24.0, ((0, 256),), (0, 1, 256, 6.0))
    out_grads = gaussian(splits[1], (TOKENS, 2, FFW), (TOK_DEV * N_MP) ** -0.5, 0.0625, ((0, 256),))
    momentum = gaussian(splits[2], (N_DP, D, 2, FFW), 1.0, 6.0, ((0, 16), (1, 16)), jnp.float32)
    selected = draw_selected(jax.random.fold_in(splits[4], 71), 0)
    return dict(tokens=tokens, out_grads=out_grads, momentum=momentum, selected=selected)


momentum_decay = 0.9
highest = lax.Precision.HIGHEST

def dct_basis(length):
    frequency = jnp.arange(length, dtype=jnp.float32)[:, None]
    position = jnp.arange(length, dtype=jnp.float32)[None, :]
    basis = jnp.cos(math.pi * (2.0 * position + 1.0) * frequency / (2.0 * length)) * math.sqrt(2.0 / length)
    scaling = jnp.where(frequency == 0.0, math.sqrt(0.5), 1.0)
    return basis * scaling

def forward_spans(values, basis):
    rows, mats, cols = values.shape
    blocks = values.reshape(rows // SPAN, SPAN, mats, cols // SPAN, SPAN)
    coeffs = jnp.einsum('ua,ramck,vk->rmcuv', basis, blocks, basis, precision=highest)
    return coeffs.reshape(rows // SPAN, mats, cols // SPAN, SPAN * SPAN)

def inverse_spans(coeffs, basis):
    crows, mats, ccols, _ = coeffs.shape
    square = coeffs.reshape(crows, mats, ccols, SPAN, SPAN)
    blocks = jnp.einsum('ua,rmcuv,vk->ramck', basis, square, basis, precision=highest)
    return blocks.reshape(crows * SPAN, mats, ccols * SPAN)

def spread_values(values, selected):
    positions = jnp.arange(SPAN * SPAN, dtype=jnp.int32)
    matches = selected[..., None] == positions
    return lax.optimization_barrier(jnp.sum(jnp.where(matches, values[..., None], 0.0), axis=-2))

def normalize(decoded):
    rows, mats, cols = decoded.shape
    view = decoded.reshape(rows // SPAN, SPAN, mats, cols // SPAN, SPAN)
    power = lax.optimization_barrier(jnp.mean(view * view, axis=(1, 4), keepdims=True))
    return (view / jnp.sqrt(power + 1e-06)).reshape(decoded.shape)

def reference(tokens, out_grads, momentum, selected):
    basis = dct_basis(SPAN)
    token_rows = tokens.reshape(N_DP, N_MP, TOK_DEV, D)
    grad_rows = out_grads.reshape(N_DP, N_MP, TOK_DEV, 2 * FFW)

    def one_replica(replica):

        def add_member(member, running):
            term = jnp.dot(token_rows[replica, member].T, grad_rows[replica, member], preferred_element_type=jnp.float32)
            return running + term
        gradient = lax.fori_loop(0, N_MP, add_member, jnp.zeros((D, 2 * FFW), jnp.float32))
        blend = momentum_decay * momentum[replica] + gradient.reshape(D, 2, FFW)
        coeffs = forward_spans(blend, basis)
        chosen = jnp.take_along_axis(coeffs, selected, axis=3)
        placed = lax.map(lambda pair: spread_values(pair[0], pair[1]), (chosen, selected))
        return (blend - inverse_spans(placed, basis), chosen)
    new_momentum, chosen_all = lax.map(one_replica, jnp.arange(N_DP, dtype=jnp.int32))
    summed = lax.optimization_barrier(jnp.sum(chosen_all, axis=0))
    filled = lax.map(lambda pair: spread_values(pair[0], pair[1]), (summed, selected))
    update = normalize(inverse_spans(filled, basis))
    return (new_momentum, update)
```

```python
import functools
import math

import jax
import jax.numpy as jnp
import numpy as np
from jax import lax
from jax.experimental import pallas as pl
from jax.experimental.pallas import tpu as pltpu
from jax.sharding import PartitionSpec as P

SPAN = 64
SIDE = 4
DECAY = 0.9
HIGHEST = lax.Precision.HIGHEST


def dct_basis(n):
    u = np.arange(n)[:, None].astype(np.float64)
    a = np.arange(n)[None, :].astype(np.float64)
    basis = np.cos(math.pi * (2.0 * a + 1.0) * u / (2.0 * n)) * math.sqrt(2.0 / n)
    basis[0] *= math.sqrt(0.5)
    return basis.astype(np.float32)


def shift_pairs(n_dp, primary, step):
    pairs = []
    n_mp = SIDE * SIDE
    for dp in range(n_dp):
        for x in range(SIDE):
            for y in range(SIDE):
                along_x = (dp % 2 == 0) == primary
                to = ((x + step) % SIDE, y) if along_x else (x, (y + step) % SIDE)
                pairs.append((dp * n_mp + x * SIDE + y, dp * n_mp + to[0] * SIDE + to[1]))
    return pairs


def matmul_kernel(table, grads_t, tokens, low, high):
    half = low.shape[-1]
    g = grads_t[...]
    low[0] = jnp.dot(g, tokens[:, :half], preferred_element_type=jnp.float32)
    high[0] = jnp.dot(g, tokens[:, half:], preferred_element_type=jnp.float32)


def partial_halves(table, grads_t, tokens, rows):
    cols, toks = grads_t.shape
    count = table.shape[0]
    half = rows // 2
    out = jax.ShapeDtypeStruct((count, cols, half), jnp.float32)
    out_spec = pl.BlockSpec((1, cols, half), lambda i, t: (i, 0, 0))
    return pl.pallas_call(
        matmul_kernel,
        grid_spec=pltpu.PrefetchScalarGridSpec(
            num_scalar_prefetch=1,
            grid=(count,),
            in_specs=[
                pl.BlockSpec((cols, toks), lambda i, t: (0, 0)),
                pl.BlockSpec((toks, rows), lambda i, t: (0, t[i])),
            ],
            out_specs=[out_spec, out_spec],
        ),
        out_shape=[out, out],
        compiler_params=pltpu.CompilerParams(vmem_limit_bytes=32 * 1024 * 1024),
        cost_estimate=pl.CostEstimate(
            flops=2 * count * rows * cols * toks,
            bytes_accessed=count * rows * (2 * toks + 4 * cols),
            transcendentals=0,
        ),
    )(table, grads_t, tokens)


def chosen_kernel(blend, left, right, chosen):
    spans = left.shape[0]
    for i in range(spans):
        x = blend[:, i * SPAN : (i + 1) * SPAN]
        w = jnp.dot(left[i], x, precision=HIGHEST, preferred_element_type=jnp.float32)
        chosen[i] = jnp.sum(w * right[i], axis=1, keepdims=True)


def decode(values, left, right, i):
    return lax.dot_general(
        left[i],
        values * right[i],
        (((0,), (0,)), ((), ())),
        precision=HIGHEST,
        preferred_element_type=jnp.float32,
    )


def momentum_kernel(blend, chosen, left, right, out):
    mats, lanes = out.shape[1], out.shape[2]
    for i in range(left.shape[0]):
        rows = slice(i * SPAN, (i + 1) * SPAN)
        new = blend[:, rows] - decode(chosen[i], left, right, i)
        for m in range(mats):
            out[rows, m, :] = new[m * lanes : (m + 1) * lanes].T


def update_kernel(gathered, left, right, out):
    mats, lanes = out.shape[1], out.shape[2]
    for i in range(left.shape[0]):
        rows = slice(i * SPAN, (i + 1) * SPAN)
        summed = jnp.sum(gathered[:, i], axis=0)
        decoded = decode(summed, left, right, i)
        cols = decoded.shape[0]
        square = (decoded * decoded).reshape(cols // SPAN, SPAN, SPAN)
        power = jnp.sum(jnp.sum(square, axis=1, keepdims=True), axis=2, keepdims=True) / (SPAN * SPAN)
        scaled = (decoded.reshape(square.shape) / jnp.sqrt(power + 1e-06)).reshape(decoded.shape)
        for m in range(mats):
            out[rows, m, :] = scaled[m * lanes : (m + 1) * lanes].T


def on_device(n_dp, tokens, out_grads, momentum, selected):
    rows, mats, lanes = momentum.shape[1:]
    cols = mats * lanes
    spans = rows // SPAN
    ccols = lanes // SPAN
    kept = selected.shape[-1]
    core = lax.axis_index("dp") % 2
    mp = lax.axis_index("mp")
    x, y = mp // SIDE, mp % SIDE
    p = jnp.where(core == 0, x, y)
    s = jnp.where(core == 0, y, x)
    away = jnp.arange(SIDE, dtype=jnp.int32)

    def blocks(dp_):
        to_p, to_s = (p + dp_) % SIDE, (s + away) % SIDE
        return jnp.where(core == 0, to_p * SIDE + to_s, to_s * SIDE + to_p).astype(jnp.int32)

    def send(v, primary, step):
        return lax.ppermute(v, ("dp", "mp"), shift_pairs(n_dp, primary, step))

    grads_t = out_grads.reshape(out_grads.shape[0], cols).T
    a_lo, a_hi = partial_halves(blocks(2), grads_t, tokens, rows)
    ra_lo = send(a_lo, True, -1)
    ra_hi = send(a_hi, True, 1)
    back_lo, back_hi = partial_halves(blocks(3), grads_t, tokens, rows)
    rb_hi = send(back_hi, True, -1)
    fore_lo, fore_hi = partial_halves(blocks(1), grads_t, tokens, rows)
    rb_lo = send(fore_lo, True, 1)
    own_lo, own_hi = partial_halves(blocks(0), grads_t, tokens, rows)
    rc_lo = send(back_lo + ra_lo, True, -1)
    rc_hi = send(fore_hi + ra_hi, True, 1)
    s_lo = [own_lo[k] + rc_lo[k] + rb_lo[k] for k in range(SIDE)]
    s_hi = [own_hi[k] + rb_hi[k] + rc_hi[k] for k in range(SIDE)]
    ta_lo = send(s_lo[2], False, -1)
    ta_hi = send(s_hi[2], False, 1)
    tb_hi = send(s_hi[3], False, -1)
    tb_lo = send(s_lo[1], False, 1)
    tc_lo = send(s_lo[3] + ta_lo, False, -1)
    tc_hi = send(s_hi[1] + ta_hi, False, 1)

    basis = jnp.asarray(dct_basis(SPAN))
    flat = selected.reshape(spans, mats * ccols * kept)
    places = jnp.arange(SPAN, dtype=jnp.int32)

    def basis_rows(index):
        hot = (index[..., None] == places).astype(jnp.float32)
        return jnp.einsum("ikp,pa->ika", hot, basis, precision=HIGHEST)

    right = basis_rows(flat // SPAN)
    narrow = basis_rows(flat % SPAN)
    group = jnp.arange(mats * ccols * kept) // kept
    column = jnp.arange(cols) // SPAN
    left = jnp.where(group[:, None] == column[None, :], jnp.tile(narrow, (1, 1, mats * ccols)), 0.0)

    faded_t = DECAY * momentum[0].reshape(rows, cols).T
    blend = faded_t + jnp.concatenate([s_lo[0] + tc_lo + tb_lo, s_hi[0] + tb_hi + tc_hi], axis=1)
    chosen = pl.pallas_call(
        chosen_kernel,
        out_shape=jax.ShapeDtypeStruct((spans, mats * ccols * kept, 1), jnp.float32),
    )(blend, left, right)
    packed = chosen.reshape(1, spans, mats * ccols * kept)
    gathered = lax.all_gather(packed, "dp", axis=0, tiled=True)[..., None]
    out_shape = jax.ShapeDtypeStruct((rows, mats, lanes), jnp.float32)
    new_momentum = pl.pallas_call(momentum_kernel, out_shape=out_shape)(blend, chosen, left, right)
    update = pl.pallas_call(update_kernel, out_shape=out_shape)(gathered, left, right)
    return new_momentum[None], update


def solution(mesh):
    return jax.shard_map(
        functools.partial(on_device, mesh.shape["dp"]),
        mesh=mesh,
        in_specs=(
            P(("dp", "mp"), None),
            P(("dp", "mp"), None, None),
            P("dp", "mp", None, None),
            P("mp", None, None, None),
        ),
        out_specs=(P("dp", "mp", None, None), P("mp", None, None)),
        check_vma=False,
    )
```

```python
import functools
import math

import jax
import jax.numpy as jnp
import numpy as np
from jax import lax
from jax.experimental import pallas as pl
from jax.experimental.pallas import tpu as pltpu
from jax.sharding import PartitionSpec as P

SPAN = 64
SIDE = 4
DECAY = 0.9
VMEM = 16 * 1024 * 1024
VMEM_LOCAL = 16 * 1024 * 1024
HIGHEST = lax.Precision.HIGHEST


def dct_basis(n):
    u = np.arange(n)[:, None].astype(np.float64)
    a = np.arange(n)[None, :].astype(np.float64)
    basis = np.cos(math.pi * (2.0 * a + 1.0) * u / (2.0 * n)) * math.sqrt(2.0 / n)
    basis[0] *= math.sqrt(0.5)
    return basis.astype(np.float32)


def swap_pairs(n_dp, primary, flip):
    pairs = []
    n_mp = SIDE * SIDE
    for dp in range(n_dp):
        for x in range(SIDE):
            for y in range(SIDE):
                along_x = (dp % 2 == 0) == primary
                to = (x ^ flip, y) if along_x else (x, y ^ flip)
                pairs.append((dp * n_mp + x * SIDE + y, dp * n_mp + to[0] * SIDE + to[1]))
    return pairs


def block_at(flip_p, flip_s):
    core = lax.axis_index("dp") % 2
    mp = lax.axis_index("mp")
    x, y = mp // SIDE, mp % SIDE
    to_p = jnp.where(core == 0, x, y) ^ flip_p
    to_s = jnp.where(core == 0, y, x) ^ flip_s
    return jnp.where(core == 0, to_p * SIDE + to_s, to_s * SIDE + to_p)


def matmul_kernel(table, grads_t, *refs):
    blocks, outs = refs[: len(refs) // 3], refs[len(refs) // 3 :]
    g = grads_t[...]
    half = outs[0].shape[-1]
    for n, block in enumerate(blocks):
        for h in range(2):
            part = block[:, h * half : (h + 1) * half]
            outs[2 * n + h][0] = jnp.dot(g, part, preferred_element_type=jnp.float32)


def partials(grads_t, tokens, rows, flips):
    cols, toks = grads_t.shape
    half = rows // 2
    groups = len(flips)
    steps = np.array([(flip, k) for flip in flips for k in range(SIDE)], np.int32)
    table = block_at(steps[:, 0], steps[:, 1]).astype(jnp.int32)

    def block(n):
        return pl.BlockSpec((toks, rows), lambda i, t: (0, t[n * SIDE + i]))

    return pl.pallas_call(
        matmul_kernel,
        grid_spec=pltpu.PrefetchScalarGridSpec(
            num_scalar_prefetch=1,
            grid=(SIDE,),
            in_specs=[pl.BlockSpec((cols, toks), lambda i, t: (0, 0))] + [block(n) for n in range(groups)],
            out_specs=[pl.BlockSpec((1, cols, half), lambda i, t: (i, 0, 0))] * (2 * groups),
        ),
        out_shape=[jax.ShapeDtypeStruct((SIDE, cols, half), jnp.float32)] * (2 * groups),
        compiler_params=pltpu.CompilerParams(vmem_limit_bytes=VMEM),
        cost_estimate=pl.CostEstimate(
            flops=2 * groups * SIDE * rows * cols * toks,
            bytes_accessed=groups * SIDE * rows * (2 * toks + 4 * cols),
            transcendentals=0,
        ),
    )(table, grads_t, *[tokens] * groups)


def halves(v):
    high = v.astype(jnp.bfloat16)
    return high, (v - high.astype(jnp.float32)).astype(jnp.bfloat16)


def dot3(a, b):
    dot = functools.partial(jnp.dot, preferred_element_type=jnp.float32)
    return dot(a[0], b[0]) + (dot(a[0], b[1]) + dot(a[1], b[0]))


def prepare_kernel(picked, up, wide, right, left_high, left_low, down_high, down_low):
    spans, kept = picked.shape
    cols = wide.shape[2]
    index = lax.broadcasted_iota(jnp.int32, (SPAN, kept), 0)
    group = kept // (cols // SPAN)

    def same(shape, col_dim):
        col = lax.broadcasted_iota(jnp.int32, shape, col_dim) // SPAN
        return col == lax.broadcasted_iota(jnp.int32, shape, 1 - col_dim) // group

    across, along = same((cols, kept), 0), same((kept, cols), 1)
    first = (((0,), (0,)), ((), ()))
    for i in range(spans):
        place = picked[i : i + 1, :]
        hot_u = (index == place >> 6).astype(jnp.float32).astype(jnp.bfloat16)
        hot_v = (index == place & (SPAN - 1)).astype(jnp.float32).astype(jnp.bfloat16)
        right[i] = jnp.dot(up[0], hot_u, preferred_element_type=jnp.float32) + jnp.dot(
            up[1], hot_u, preferred_element_type=jnp.float32
        )
        for part, (left, down) in enumerate(((left_high, down_high), (left_low, down_low))):
            v = lax.dot_general(wide[part], hot_v, first, preferred_element_type=jnp.float32)
            left[i] = jnp.where(across, v, 0.0).astype(jnp.bfloat16)
            if i < down.shape[0]:
                v = lax.dot_general(hot_v, wide[part], first, preferred_element_type=jnp.float32)
                down[i] = jnp.where(along, v, 0.0).astype(jnp.bfloat16)


def fade_kernel(momentum, faded):
    lanes = momentum.shape[2]
    for m in range(momentum.shape[1]):
        faded[:, m * lanes : (m + 1) * lanes] = DECAY * momentum[:, m, :]


def total_of(parts, faded, step, h):
    half = faded.shape[0] // 2
    total = (parts[h][0][step] + parts[h][1][step] + parts[h][2][step]).T
    return total if step else total + faded[h * half : (h + 1) * half, :]


def kept_kernel(parts, faded, right, left_high, left_low, *chosen):
    rows = faded.shape[0]
    spans = rows // SPAN
    for step in range(SIDE):
        for h in range(2):
            total = total_of(parts, faded, step, h)
            for j in range(spans // 2):
                i = h * (spans // 2) + j
                n = step * spans + i
                values = halves(total[j * SPAN : (j + 1) * SPAN, :])
                w = dot3(values, (left_high[n], left_low[n]))
                chosen[step][i : i + 1, :] = jnp.sum(w * right[n], axis=0, keepdims=True)


def join_kernel(parts, faded, *joined):
    half = faded.shape[0] // 2
    for step in range(SIDE):
        for h in range(2):
            joined[step][h * half : (h + 1) * half, :] = total_of(parts, faded, step, h)


def decode(values, right, down_high, down_low, i):
    return dot3(halves(right[i] * values[i : i + 1, :]), (down_high[i], down_low[i]))


def rest_kernel(joined, chosen, right, down_high, down_low, rest):
    for i in range(down_high.shape[0]):
        rows = slice(i * SPAN, (i + 1) * SPAN)
        rest[rows, :] = joined[rows, :] - decode(chosen, right, down_high, down_low, i)


def last_kernel(pieces, mine, other, right, down_high, down_low, momentum, update):
    mats, lanes = update.shape[1], update.shape[2]
    cols = mats * lanes
    spans = down_high.shape[0]
    summed = mine[...] + other[...]
    decoded = [decode(summed, right, down_high, down_low, i) for i in range(spans)]
    squares = jnp.concatenate([jnp.sum(d * d, axis=0, keepdims=True) for d in decoded], axis=0)
    same = lax.broadcasted_iota(jnp.int32, (cols, cols), 0) // SPAN == (
        lax.broadcasted_iota(jnp.int32, (cols, cols), 1) // SPAN
    )
    power = jnp.dot(
        squares, same.astype(jnp.float32), precision=HIGHEST, preferred_element_type=jnp.float32
    ) / (SPAN * SPAN)
    scale = 1.0 / jnp.sqrt(power + 1e-06)
    for i in range(spans):
        rows = slice(i * SPAN, (i + 1) * SPAN)
        scaled = decoded[i] * scale[i : i + 1, :]
        new = pieces[0][rows, :]
        for piece in pieces[1:]:
            new = new + piece[rows, :]
        for m in range(mats):
            there = slice(m * lanes, (m + 1) * lanes)
            update[rows, m, :] = scaled[:, there]
            momentum[rows, m, :] = new[:, there]


def local(kernel, out_shape, **specs):
    return pl.pallas_call(
        kernel,
        out_shape=out_shape,
        **specs,
        compiler_params=pltpu.CompilerParams(vmem_limit_bytes=VMEM_LOCAL),
    )


def on_device(n_dp, tokens, out_grads, momentum, selected):
    rows, mats, lanes = momentum.shape[1:]
    cols = mats * lanes
    spans = rows // SPAN
    ccols = lanes // SPAN
    kept = selected.shape[-1]
    def send(v, primary, flip):
        return lax.ppermute(v, ("dp", "mp"), swap_pairs(n_dp, primary, flip))

    grads_t = out_grads.reshape(out_grads.shape[0], cols).T
    a_lo, a_hi = partials(grads_t, tokens, rows, (2,))
    ra_lo, ra_hi = send(a_lo, True, 1), send(a_hi, True, 3)
    slots = mats * ccols * kept
    picked, _ = lax.optimization_barrier((selected.reshape(spans, slots), a_lo))
    picked = jnp.concatenate([picked, send(picked, False, 1)])
    near_lo, near_hi, far_lo, far_hi = partials(grads_t, tokens, rows, (1, 3))
    rb_lo = send(near_lo, True, 1)
    rb_hi = send(far_hi, True, 3)
    picked = jnp.concatenate([picked, send(picked, False, 2)])
    own_lo, own_hi = partials(grads_t, tokens, rows, (0,))
    rc_hi = send(near_hi + ra_hi, True, 1)
    rc_lo = send(far_lo + ra_lo, True, 3)
    f32, b16 = jnp.float32, jnp.bfloat16
    basis = dct_basis(SPAN)

    def constant_halves(v):
        high = v.astype(b16)
        return jnp.asarray(np.stack([high, (v - high.astype(np.float32)).astype(b16)]))

    right, left_high, left_low, down_high, down_low = local(
        prepare_kernel,
        [jax.ShapeDtypeStruct((SIDE * spans, SPAN, slots), f32)]
        + [jax.ShapeDtypeStruct((SIDE * spans, cols, slots), b16)] * 2
        + [jax.ShapeDtypeStruct((spans, slots, cols), b16)] * 2,
    )(picked, constant_halves(basis.T), constant_halves(np.tile(basis, (1, cols // SPAN))))
    faded = local(fade_kernel, jax.ShapeDtypeStruct((rows, cols), f32))(momentum[0])
    parts = [[own_lo, rb_lo, rc_lo], [own_hi, rb_hi, rc_hi]]
    chosen = local(kept_kernel, [jax.ShapeDtypeStruct((spans, slots), f32)] * SIDE)(
        parts, faded, right, left_high, left_low
    )
    came = [send(chosen[step], False, step) for step in (2, 1, 3)]
    joined = local(join_kernel, [jax.ShapeDtypeStruct((rows, cols), f32)] * SIDE)(parts, faded)
    pieces = [joined[0]]
    chosen = total = chosen[0] + came[0] + came[1] + came[2]
    for flip, behind in ((1, (2,)), (2, (1, 3)), (4, ()), (12, ())):
        other = lax.ppermute(total, "dp", [(i, i ^ flip) for i in range(n_dp)])
        for step in behind:
            block, _ = lax.optimization_barrier((joined[step], total))
            pieces.append(send(block, False, step))
        mine, total = total, total + other
    out_shape = jax.ShapeDtypeStruct((rows, mats, lanes), f32)
    pieces[0] = local(rest_kernel, jax.ShapeDtypeStruct((rows, cols), f32))(
        joined[0], chosen, right, down_high, down_low
    )
    new_momentum, update = local(last_kernel, [out_shape, out_shape])(
        pieces, mine, other, right, down_high, down_low
    )
    return new_momentum[None], update


def solution(mesh):
    return jax.shard_map(
        functools.partial(on_device, mesh.shape["dp"]),
        mesh=mesh,
        in_specs=(
            P(("dp", "mp"), None),
            P(("dp", "mp"), None, None),
            P("dp", "mp", None, None),
            P("mp", None, None, None),
        ),
        out_specs=(P("dp", "mp", None, None), P("mp", None, None)),
        check_vma=False,
    )
```

```python
import functools
import math

import jax
import jax.numpy as jnp
import numpy as np
from jax import lax
from jax.experimental import pallas as pl
from jax.experimental.pallas import tpu as pltpu
from jax.sharding import PartitionSpec as P

SPAN = 64
SIDE = 4
ORDER = (1, 2, 3, 0)
DECAY = 0.9
VMEM = 20 * 1024 * 1024
VMEM_LOCAL = 16 * 1024 * 1024
HIGHEST = lax.Precision.HIGHEST


def dct_basis(n):
    u = np.arange(n)[:, None].astype(np.float64)
    a = np.arange(n)[None, :].astype(np.float64)
    basis = np.cos(math.pi * (2.0 * a + 1.0) * u / (2.0 * n)) * math.sqrt(2.0 / n)
    basis[0] *= math.sqrt(0.5)
    return basis.astype(np.float32)


def swap_pairs(n_dp, primary, flip):
    pairs = []
    n_mp = SIDE * SIDE
    for dp in range(n_dp):
        for x in range(SIDE):
            for y in range(SIDE):
                along_x = (dp % 2 == 0) == primary
                to = (x ^ flip, y) if along_x else (x, y ^ flip)
                pairs.append((dp * n_mp + x * SIDE + y, dp * n_mp + to[0] * SIDE + to[1]))
    return pairs


def block_at(flip_p, flip_s):
    core = lax.axis_index("dp") % 2
    mp = lax.axis_index("mp")
    x, y = mp // SIDE, mp % SIDE
    to_p = jnp.where(core == 0, x, y) ^ flip_p
    to_s = jnp.where(core == 0, y, x) ^ flip_s
    return jnp.where(core == 0, to_p * SIDE + to_s, to_s * SIDE + to_p)


def matmul_kernel(groups, grads_t, tokens, *outs):
    half = outs[0].shape[-1]
    for n, group in enumerate(groups):
        for i, flips in enumerate(group):
            for h in range(2):
                start = (2 * block_at(*flips) + h) * half
                part = tokens[:, pl.ds(pl.multiple_of(start, half), half)]
                outs[2 * n + h][i] = jnp.dot(grads_t[...], part, preferred_element_type=jnp.float32)


def partials(grads_t, tokens, rows, groups):
    cols, toks = grads_t.shape
    count = sum(map(len, groups))
    return pl.pallas_call(
        functools.partial(matmul_kernel, groups),
        out_shape=[
            jax.ShapeDtypeStruct((len(group), cols, rows // 2), jnp.float32) for group in groups for _ in range(2)
        ],
        compiler_params=pltpu.CompilerParams(vmem_limit_bytes=VMEM),
        cost_estimate=pl.CostEstimate(
            flops=2 * count * rows * cols * toks,
            bytes_accessed=count * rows * (2 * toks + 4 * cols),
            transcendentals=0,
        ),
    )(grads_t, tokens)


def halves(v):
    high = v.astype(jnp.bfloat16)
    return high, (v - high.astype(jnp.float32)).astype(jnp.bfloat16)


def dot3(a, b):
    dot = functools.partial(jnp.dot, preferred_element_type=jnp.float32)
    return dot(a[0], b[0]) + (dot(a[0], b[1]) + dot(a[1], b[0]))


def prepare_kernel(picked, up, wide, right, left_high, left_low, down_high, down_low):
    spans, kept = picked.shape
    cols = wide.shape[2]
    index = lax.broadcasted_iota(jnp.int32, (SPAN, kept), 0)
    group = kept // (cols // SPAN)

    def same(shape, col_dim):
        col = lax.broadcasted_iota(jnp.int32, shape, col_dim) // SPAN
        return col == lax.broadcasted_iota(jnp.int32, shape, 1 - col_dim) // group

    across, along = same((cols, kept), 0), same((kept, cols), 1)
    first = (((0,), (0,)), ((), ()))
    for i in range(spans):
        place = picked[i : i + 1, :]
        hot_u = (index == place >> 6).astype(jnp.float32).astype(jnp.bfloat16)
        hot_v = (index == place & (SPAN - 1)).astype(jnp.float32).astype(jnp.bfloat16)
        right[i] = jnp.dot(up[0], hot_u, preferred_element_type=jnp.float32) + jnp.dot(
            up[1], hot_u, preferred_element_type=jnp.float32
        )
        for part, (left, down) in enumerate(((left_high, down_high), (left_low, down_low))):
            v = lax.dot_general(wide[part], hot_v, first, preferred_element_type=jnp.float32)
            left[i] = jnp.where(across, v, 0.0).astype(jnp.bfloat16)
            if i < down.shape[0]:
                v = lax.dot_general(hot_v, wide[part], first, preferred_element_type=jnp.float32)
                down[i] = jnp.where(along, v, 0.0).astype(jnp.bfloat16)


def fade_kernel(momentum, faded):
    lanes = momentum.shape[2]
    for m in range(momentum.shape[1]):
        faded[:, m * lanes : (m + 1) * lanes] = DECAY * momentum[:, m, :]


def keep(total, n, i, right, left_high, left_low, chosen):
    for j in range(total.shape[0] // SPAN):
        values = halves(total[j * SPAN : (j + 1) * SPAN, :])
        w = dot3(values, (left_high[n + i + j], left_low[n + i + j]))
        chosen[i + j : i + j + 1, :] = jnp.sum(w * right[n + i + j], axis=0, keepdims=True)


def join_kernel(parts, right, left_high, left_low, joined, chosen):
    spans = chosen[0].shape[0]
    for step, out in enumerate(chosen):
        half = joined[step].shape[0] // 2
        for h in range(2):
            total = (parts[h][0][step] + parts[h][1][step] + parts[h][2][step]).T
            joined[step][h * half : (h + 1) * half, :] = total
            keep(total, (step + 1) * spans, h * (spans // 2), right, left_high, left_low, out)


def late_kernel(low, high, came_low, came_high, out_near, out_far):
    out_near[0] = low[SIDE]
    out_near[1] = high[SIDE] + came_high[SIDE - 1]
    out_far[0] = high[SIDE + 1]
    out_far[1] = low[SIDE + 1] + came_low[SIDE - 1]


def own_kernel(parts, faded, right, left_high, left_low, joined, chosen):
    rows = faded.shape[0]
    half = rows // 2
    for h in range(2):
        own, near, far = parts[0][h], parts[1], parts[2]
        total = (own[SIDE - 1] + near[h] + far[1 - h]).T + faded[h * half : (h + 1) * half, :]
        joined[h * half : (h + 1) * half, :] = total
        keep(total, 0, h * (chosen.shape[0] // 2), right, left_high, left_low, chosen)


def decode(values, right, down_high, down_low, i):
    return dot3(halves(right[i] * values[i : i + 1, :]), (down_high[i], down_low[i]))


def rest_kernel(joined, chosen, right, down_high, down_low, rest):
    for i in range(down_high.shape[0]):
        rows = slice(i * SPAN, (i + 1) * SPAN)
        rest[rows, :] = joined[rows, :] - decode(chosen, right, down_high, down_low, i)


def last_kernel(pieces, mine, other, right, down_high, down_low, momentum, update):
    mats, lanes = update.shape[1], update.shape[2]
    cols = mats * lanes
    spans = down_high.shape[0]
    summed = mine[...] + other[...]
    decoded = [decode(summed, right, down_high, down_low, i) for i in range(spans)]
    squares = jnp.concatenate([jnp.sum(d * d, axis=0, keepdims=True) for d in decoded], axis=0)
    same = lax.broadcasted_iota(jnp.int32, (cols, cols), 0) // SPAN == (
        lax.broadcasted_iota(jnp.int32, (cols, cols), 1) // SPAN
    )
    power = jnp.dot(
        squares, same.astype(jnp.float32), precision=HIGHEST, preferred_element_type=jnp.float32
    ) / (SPAN * SPAN)
    scale = 1.0 / jnp.sqrt(power + 1e-06)
    for i in range(spans):
        rows = slice(i * SPAN, (i + 1) * SPAN)
        scaled = decoded[i] * scale[i : i + 1, :]
        new = pieces[0][rows, :]
        for piece in pieces[1:]:
            new = new + piece[rows, :]
        for m in range(mats):
            there = slice(m * lanes, (m + 1) * lanes)
            update[rows, m, :] = scaled[:, there]
            momentum[rows, m, :] = new[:, there]


def local(kernel, out_shape, **specs):
    return pl.pallas_call(
        kernel,
        out_shape=out_shape,
        **specs,
        compiler_params=pltpu.CompilerParams(vmem_limit_bytes=VMEM_LOCAL),
    )


def on_device(n_dp, tokens, out_grads, momentum, selected):
    rows, mats, lanes = momentum.shape[1:]
    cols = mats * lanes
    spans = rows // SPAN
    ccols = lanes // SPAN
    kept = selected.shape[-1]
    def send(v, primary, flip):
        return lax.ppermute(v, ("dp", "mp"), swap_pairs(n_dp, primary, flip))

    grads_t = out_grads.reshape(out_grads.shape[0], cols).T
    def blocks(flip, seconds=ORDER):
        return [(flip, k) for k in seconds]

    a_lo, a_hi = partials(grads_t, tokens, rows, [blocks(2)])
    ra_lo, ra_hi = send(a_lo, True, 1), send(a_hi, True, 3)
    near_lo, near_hi, far_lo, far_hi, own_lo, own_hi = partials(
        grads_t,
        tokens,
        rows,
        [
            blocks(1, ORDER[:-1]),
            blocks(3, ORDER[:-1]),
            blocks(0) + [(1, ORDER[-1]), (3, ORDER[-1])],
        ],
    )
    rb_lo = send(near_lo, True, 1)
    rb_hi = send(far_hi, True, 3)
    slots = mats * ccols * kept
    picked, _ = lax.optimization_barrier((selected.reshape(spans, slots), near_lo))
    picked = jnp.concatenate([picked, send(picked, False, 1)])
    near_hi, far_lo, picked = lax.optimization_barrier((near_hi, far_lo, picked))
    picked = jnp.concatenate([picked, send(picked, False, 2)])
    rc_hi = send(near_hi + ra_hi[: SIDE - 1], True, 1)
    rc_lo = send(far_lo + ra_lo[: SIDE - 1], True, 3)
    f32, b16 = jnp.float32, jnp.bfloat16
    basis = dct_basis(SPAN)

    def constant_halves(v):
        high = v.astype(b16)
        return jnp.asarray(np.stack([high, (v - high.astype(np.float32)).astype(b16)]))

    right, left_high, left_low, down_high, down_low = local(
        prepare_kernel,
        [jax.ShapeDtypeStruct((SIDE * spans, SPAN, slots), f32)]
        + [jax.ShapeDtypeStruct((SIDE * spans, cols, slots), b16)] * 2
        + [jax.ShapeDtypeStruct((spans, slots, cols), b16)] * 2,
    )(picked, constant_halves(basis.T), constant_halves(np.tile(basis, (1, cols // SPAN))))
    faded = local(fade_kernel, jax.ShapeDtypeStruct((rows, cols), f32))(momentum[0])
    own_lo, own_hi, right, faded = lax.optimization_barrier((own_lo, own_hi, right, faded))
    late_shape = jax.ShapeDtypeStruct((2, cols, rows // 2), f32)
    late_near, late_far = local(late_kernel, [late_shape] * 2)(own_lo, own_hi, ra_lo, ra_hi)
    rf_near = send(late_near, True, 1)
    rf_far = send(late_far, True, 3)
    parts = [[own_lo, rb_lo, rc_lo], [own_hi, rb_hi, rc_hi]]
    joined, chosen = local(
        join_kernel,
        [
            [jax.ShapeDtypeStruct((rows, cols), f32)] * (SIDE - 1),
            [jax.ShapeDtypeStruct((spans, slots), f32)] * (SIDE - 1),
        ],
    )(parts, right, left_high, left_low)
    came = [send(chosen[flip - 1], False, flip) for flip in (2, 1, 3)]
    own, chosen = local(
        own_kernel,
        [jax.ShapeDtypeStruct((rows, cols), f32), jax.ShapeDtypeStruct((spans, slots), f32)],
    )([[own_lo, own_hi], rf_near, rf_far], faded, right, left_high, left_low)
    chosen = total = chosen + came[0] + came[1] + came[2]
    pieces = [None]
    for flip, behind in ((1, (2,)), (2, (1, 3)), (4, ()), (12, ())):
        other = lax.ppermute(total, "dp", [(i, i ^ flip) for i in range(n_dp)])
        for step in behind:
            block, _ = lax.optimization_barrier((joined[step - 1], total))
            pieces.append(send(block, False, step))
        mine, total = total, total + other
    out_shape = jax.ShapeDtypeStruct((rows, mats, lanes), f32)
    pieces[0] = local(rest_kernel, jax.ShapeDtypeStruct((rows, cols), f32))(
        own, chosen, right, down_high, down_low
    )
    new_momentum, update = local(last_kernel, [out_shape, out_shape])(
        pieces, mine, other, right, down_high, down_low
    )
    return new_momentum[None], update


def solution(mesh):
    return jax.shard_map(
        functools.partial(on_device, mesh.shape["dp"]),
        mesh=mesh,
        in_specs=(
            P(("dp", "mp"), None),
            P(("dp", "mp"), None, None),
            P("dp", "mp", None, None),
            P("mp", None, None, None),
        ),
        out_specs=(P("dp", "mp", None, None), P("mp", None, None)),
        check_vma=False,
    )
```

```python
import functools
import math

import jax
import jax.numpy as jnp
import numpy as np
from jax import lax
from jax.experimental import pallas as pl
from jax.experimental.pallas import tpu as pltpu
from jax.sharding import PartitionSpec as P

SPAN = 64
SIDE = 4
ORDER = (1, 2, 3, 0)
DECAY = 0.9
VMEM = 20 * 1024 * 1024
VMEM_LOCAL = 16 * 1024 * 1024
HIGHEST = lax.Precision.HIGHEST


def dct_basis(n):
    u = np.arange(n)[:, None].astype(np.float64)
    a = np.arange(n)[None, :].astype(np.float64)
    basis = np.cos(math.pi * (2.0 * a + 1.0) * u / (2.0 * n)) * math.sqrt(2.0 / n)
    basis[0] *= math.sqrt(0.5)
    return basis.astype(np.float32)


def swap_pairs(n_dp, primary, flip):
    pairs = []
    n_mp = SIDE * SIDE
    for dp in range(n_dp):
        for x in range(SIDE):
            for y in range(SIDE):
                along_x = (dp % 2 == 0) == primary
                to = (x ^ flip, y) if along_x else (x, y ^ flip)
                pairs.append((dp * n_mp + x * SIDE + y, dp * n_mp + to[0] * SIDE + to[1]))
    return pairs


def block_at(flip_p, flip_s):
    core = lax.axis_index("dp") % 2
    mp = lax.axis_index("mp")
    x, y = mp // SIDE, mp % SIDE
    to_p = jnp.where(core == 0, x, y) ^ flip_p
    to_s = jnp.where(core == 0, y, x) ^ flip_s
    return jnp.where(core == 0, to_p * SIDE + to_s, to_s * SIDE + to_p)


def matmul_kernel(groups, grads_t, tokens, *outs):
    half = outs[0].shape[-1]
    for n, group in enumerate(groups):
        for i, flips in enumerate(group):
            for h in range(2):
                start = (2 * block_at(*flips) + h) * half
                part = tokens[:, pl.ds(pl.multiple_of(start, half), half)]
                outs[2 * n + h][i] = jnp.dot(grads_t[...], part, preferred_element_type=jnp.float32)


def partials(grads_t, tokens, rows, groups):
    cols, toks = grads_t.shape
    count = sum(map(len, groups))
    return pl.pallas_call(
        functools.partial(matmul_kernel, groups),
        out_shape=[
            jax.ShapeDtypeStruct((len(group), cols, rows // 2), jnp.float32) for group in groups for _ in range(2)
        ],
        compiler_params=pltpu.CompilerParams(vmem_limit_bytes=VMEM),
        cost_estimate=pl.CostEstimate(
            flops=2 * count * rows * cols * toks,
            bytes_accessed=count * rows * (2 * toks + 4 * cols),
            transcendentals=0,
        ),
    )(grads_t, tokens)


def halves(v):
    high = v.astype(jnp.bfloat16)
    return high, (v - high.astype(jnp.float32)).astype(jnp.bfloat16)


def dot3(a, b):
    dot = functools.partial(jnp.dot, preferred_element_type=jnp.float32)
    return dot(a[0], b[0]) + (dot(a[0], b[1]) + dot(a[1], b[0]))


def prepare_kernel(picked, up, wide, right, left_high, left_low, down_high, down_low):
    spans, kept = picked.shape
    cols = wide.shape[2]
    index = lax.broadcasted_iota(jnp.int32, (SPAN, kept), 0)
    group = kept // (cols // SPAN)

    def same(shape, col_dim):
        col = lax.broadcasted_iota(jnp.int32, shape, col_dim) // SPAN
        return col == lax.broadcasted_iota(jnp.int32, shape, 1 - col_dim) // group

    across, along = same((cols, kept), 0), same((kept, cols), 1)
    first = (((0,), (0,)), ((), ()))
    for i in range(spans):
        place = picked[i : i + 1, :]
        hot_u = (index == place >> 6).astype(jnp.float32).astype(jnp.bfloat16)
        hot_v = (index == place & (SPAN - 1)).astype(jnp.float32).astype(jnp.bfloat16)
        right[i] = jnp.dot(up[0], hot_u, preferred_element_type=jnp.float32) + jnp.dot(
            up[1], hot_u, preferred_element_type=jnp.float32
        )
        for part, (left, down) in enumerate(((left_high, down_high), (left_low, down_low))):
            v = lax.dot_general(wide[part], hot_v, first, preferred_element_type=jnp.float32)
            left[i] = jnp.where(across, v, 0.0).astype(jnp.bfloat16)
            if i < down.shape[0]:
                v = lax.dot_general(hot_v, wide[part], first, preferred_element_type=jnp.float32)
                down[i] = jnp.where(along, v, 0.0).astype(jnp.bfloat16)


def fade_kernel(momentum, faded):
    lanes = momentum.shape[2]
    for m in range(momentum.shape[1]):
        faded[:, m * lanes : (m + 1) * lanes] = DECAY * momentum[:, m, :]


def keep(total, n, i, right, left_high, left_low, chosen):
    for j in range(total.shape[0] // SPAN):
        values = halves(total[j * SPAN : (j + 1) * SPAN, :])
        w = dot3(values, (left_high[n + i + j], left_low[n + i + j]))
        chosen[i + j : i + j + 1, :] = jnp.sum(w * right[n + i + j], axis=0, keepdims=True)


def join_kernel(parts, right, left_high, left_low, joined, chosen):
    spans = chosen[0].shape[0]
    for step, out in enumerate(chosen):
        half = joined[step].shape[0] // 2
        for h in range(2):
            total = (parts[h][0][step] + parts[h][1][step] + parts[h][2][step]).T
            joined[step][h * half : (h + 1) * half, :] = total
            keep(total, (step + 1) * spans, h * (spans // 2), right, left_high, left_low, out)


def late_kernel(low, high, came_low, came_high, out_near, out_far):
    out_near[0] = low[SIDE]
    out_near[1] = high[SIDE] + came_high[SIDE - 1]
    out_far[0] = high[SIDE + 1]
    out_far[1] = low[SIDE + 1] + came_low[SIDE - 1]


def own_kernel(parts, faded, right, left_high, left_low, joined, chosen):
    rows = faded.shape[0]
    half = rows // 2
    for h in range(2):
        own, near, far = parts[0][h], parts[1], parts[2]
        total = (own[SIDE - 1] + near[h] + far[1 - h]).T + faded[h * half : (h + 1) * half, :]
        joined[h * half : (h + 1) * half, :] = total
        keep(total, 0, h * (chosen.shape[0] // 2), right, left_high, left_low, chosen)


def decode(values, right, down_high, down_low, i):
    return dot3(halves(right[i] * values[i : i + 1, :]), (down_high[i], down_low[i]))


def rest_kernel(joined, chosen, right, down_high, down_low, rest):
    for i in range(down_high.shape[0]):
        rows = slice(i * SPAN, (i + 1) * SPAN)
        rest[rows, :] = joined[rows, :] - decode(chosen, right, down_high, down_low, i)


def last_kernel(pieces, mine, other, right, down_high, down_low, momentum, update):
    mats, lanes = update.shape[1], update.shape[2]
    cols = mats * lanes
    spans = down_high.shape[0]
    summed = mine[...] + other[...]
    decoded = [decode(summed, right, down_high, down_low, i) for i in range(spans)]
    squares = jnp.concatenate([jnp.sum(d * d, axis=0, keepdims=True) for d in decoded], axis=0)
    same = lax.broadcasted_iota(jnp.int32, (cols, cols), 0) // SPAN == (
        lax.broadcasted_iota(jnp.int32, (cols, cols), 1) // SPAN
    )
    power = jnp.dot(
        squares, same.astype(jnp.float32), precision=HIGHEST, preferred_element_type=jnp.float32
    ) / (SPAN * SPAN)
    scale = 1.0 / jnp.sqrt(power + 1e-06)
    for i in range(spans):
        rows = slice(i * SPAN, (i + 1) * SPAN)
        scaled = decoded[i] * scale[i : i + 1, :]
        new = pieces[0][rows, :]
        for piece in pieces[1:]:
            new = new + piece[rows, :]
        for m in range(mats):
            there = slice(m * lanes, (m + 1) * lanes)
            update[rows, m, :] = scaled[:, there]
            momentum[rows, m, :] = new[:, there]


def local(kernel, out_shape, **specs):
    return pl.pallas_call(
        kernel,
        out_shape=out_shape,
        **specs,
        compiler_params=pltpu.CompilerParams(vmem_limit_bytes=VMEM_LOCAL),
    )


def on_device(n_dp, tokens, out_grads, momentum, selected):
    rows, mats, lanes = momentum.shape[1:]
    cols = mats * lanes
    spans = rows // SPAN
    ccols = lanes // SPAN
    kept = selected.shape[-1]
    def send(v, primary, flip):
        return lax.ppermute(v, ("dp", "mp"), swap_pairs(n_dp, primary, flip))

    grads_t = out_grads.reshape(out_grads.shape[0], cols).T
    def blocks(flip, seconds=ORDER):
        return [(flip, k) for k in seconds]

    a_lo, a_hi = partials(grads_t, tokens, rows, [blocks(2)])
    ra_lo, ra_hi = send(a_lo, True, 1), send(a_hi, True, 3)
    near_lo, near_hi, far_lo, far_hi, own_lo, own_hi = partials(
        grads_t,
        tokens,
        rows,
        [
            blocks(1, ORDER[:-1]),
            blocks(3, ORDER[:-1]),
            blocks(0) + [(1, ORDER[-1]), (3, ORDER[-1])],
        ],
    )
    rb_lo = send(near_lo, True, 1)
    rb_hi = send(far_hi, True, 3)
    slots = mats * ccols * kept
    picked, _ = lax.optimization_barrier((selected.reshape(spans, slots), near_lo))
    picked = jnp.concatenate([picked, send(picked, False, 1)])
    near_hi, far_lo, picked = lax.optimization_barrier((near_hi, far_lo, picked))
    picked = jnp.concatenate([picked, send(picked, False, 2)])
    rc_hi = send(near_hi + ra_hi[: SIDE - 1], True, 1)
    rc_lo = send(far_lo + ra_lo[: SIDE - 1], True, 3)
    f32, b16 = jnp.float32, jnp.bfloat16
    basis = dct_basis(SPAN)

    def constant_halves(v):
        high = v.astype(b16)
        return jnp.asarray(np.stack([high, (v - high.astype(np.float32)).astype(b16)]))

    right, left_high, left_low, down_high, down_low = local(
        prepare_kernel,
        [jax.ShapeDtypeStruct((SIDE * spans, SPAN, slots), f32)]
        + [jax.ShapeDtypeStruct((SIDE * spans, cols, slots), b16)] * 2
        + [jax.ShapeDtypeStruct((spans, slots, cols), b16)] * 2,
    )(picked, constant_halves(basis.T), constant_halves(np.tile(basis, (1, cols // SPAN))))
    faded = local(fade_kernel, jax.ShapeDtypeStruct((rows, cols), f32))(momentum[0])
    own_lo, own_hi, right, faded = lax.optimization_barrier((own_lo, own_hi, right, faded))
    late_shape = jax.ShapeDtypeStruct((2, cols, rows // 2), f32)
    late_near, late_far = local(late_kernel, [late_shape] * 2)(own_lo, own_hi, ra_lo, ra_hi)
    rf_near = send(late_near, True, 1)
    rf_far = send(late_far, True, 3)
    parts = [[own_lo, rb_lo, rc_lo], [own_hi, rb_hi, rc_hi]]
    joined, chosen = local(
        join_kernel,
        [
            [jax.ShapeDtypeStruct((rows, cols), f32)] * (SIDE - 1),
            [jax.ShapeDtypeStruct((spans, slots), f32)] * (SIDE - 1),
        ],
    )(parts, right, left_high, left_low)
    came = [send(chosen[flip - 1], False, flip) for flip in (2, 1, 3)]
    own, chosen = local(
        own_kernel,
        [jax.ShapeDtypeStruct((rows, cols), f32), jax.ShapeDtypeStruct((spans, slots), f32)],
    )([[own_lo, own_hi], rf_near, rf_far], faded, right, left_high, left_low)
    chosen = total = chosen + came[0] + came[1] + came[2]
    pieces = [None]
    for flip, behind in ((1, (2, 1)), (2, ()), (4, (3,)), (12, ())):
        other = lax.ppermute(total, "dp", [(i, i ^ flip) for i in range(n_dp)])
        for step in behind:
            block, _ = lax.optimization_barrier((joined[step - 1], total))
            pieces.append(send(block, False, step))
        mine, total = total, total + other
    out_shape = jax.ShapeDtypeStruct((rows, mats, lanes), f32)
    pieces[0] = local(rest_kernel, jax.ShapeDtypeStruct((rows, cols), f32))(
        own, chosen, right, down_high, down_low
    )
    new_momentum, update = local(last_kernel, [out_shape, out_shape])(
        pieces, mine, other, right, down_high, down_low
    )
    return new_momentum[None], update


def solution(mesh):
    return jax.shard_map(
        functools.partial(on_device, mesh.shape["dp"]),
        mesh=mesh,
        in_specs=(
            P(("dp", "mp"), None),
            P(("dp", "mp"), None, None),
            P("dp", "mp", None, None),
            P("mp", None, None, None),
        ),
        out_specs=(P("dp", "mp", None, None), P("mp", None, None)),
        check_vma=False,
    )
```
